128 devices in a mesh: section: 2 (over core), expert: 64 (over z, y, x), dp: 1.
Axes of the slice: x: 4, y: 4, z: 4, core: 2. Of those that a mesh axis runs over, the one named last changes fastest.
Arguments:
- w_up: bfloat16 [2, 32768, 1536], P('section', 'expert'), may hold values from -0.15625 to 0.15625
- saved_rows: bfloat16 [2, 4096, 2048], P('section', ('dp', 'expert')), may hold values from -6 to 6
- hidden_grad: bfloat16 [2, 4096, 8, 1536], P('section', ('dp', 'expert')), may hold values from -6 to 6
- expert_ids: int32 [2, 4096, 8], P('section', ('dp', 'expert')), may hold values from 0 to 15, all different within a row; in each aligned block of 64 rows (0 to 63, 64 to 127, ..., all dimensions but the last counted through in order) at most 48 rows name the same one
- route_weight: float32 [2, 4096, 8], P('section', ('dp', 'expert')), may hold values from 0.1 to 1
Outputs:
- weight_grad: bfloat16 [2, 32768, 1536], P('section', ('dp', 'expert'))
- upstream: bfloat16 [2, 4096, 2048], P('section', ('dp', 'expert'))
The draws below stay inside these ranges and needn't reach their ends.
Inputs may be any that keep to these rules, and one draw needn't show every extreme that they name: `expert_ids`: each token names 8 different experts. In each aligned block of 64 tokens of a segment (the tokens of one device), no expert is chosen by more than 48 tokens, and in some block one expert is chosen by exactly 48.
All inputs are finite; a program needn't handle non-finite values.
Results may differ from the reference program's by a relative error of at most 0.0057.
Values may be sent and summed in bfloat16 or wider, within the bound.
No kernel may reach another device: no remote copies, remote signals or barrier semaphores. Data moves between devices by JAX's collectives and lax.ppermute only.
A program may use at most 128 MiB of HBM per device.

```python
import math
import jax
import jax.numpy as jnp
import numpy as np
from jax import lax

DW = 2048
FF = 1536
TOK = 64
SECTIONS = 2
EXPERTS = 16
TOPK = 8
CAP = 48
TOKENS = 4096


def level_of(rng, extent, cuts, least, high):
    gain = 1.0
    for dim, blocks in cuts:
        steps = jax.random.uniform(jax.random.fold_in(jax.random.fold_in(rng, 6), dim), (blocks,), jnp.float32, least / len(cuts), high / len(cuts))
        gain = gain * jnp.repeat(jnp.exp(steps), extent[dim] // blocks).reshape((-1,) + (1,) * (len(extent) - 1 - dim))
    return gain


def deal_out(own_key, own, number, rows, amount, top, limit, lean):
    order = jax.random.permutation(own_key, amount)
    heavy_load, usual = shares(amount, rows * top, limit, lean, True), shares(amount, rows * top, limit, lean, False)
    places = jnp.arange(amount)

    def named(tallies, rotation):
        used = int((tallies > 0).sum())
        fixed = max(1, used // 4)
        moved = fixed + (places - fixed + rotation * (used - fixed)) % max(1, amount - fixed)
        return jnp.zeros((amount,), jnp.int32).at[order[jnp.where(places < fixed, places, moved)]].set(jnp.asarray(tallies, jnp.int32))

    tallies = jnp.where(number % 4 == 0, named(heavy_load, number // 4), named(usual, number - number // 4 - 1))
    mixed = jax.random.permutation(jax.random.fold_in(own, 3), amount)
    giver, receiver = mixed[0:amount // 2 * 2:2], mixed[1:amount // 2 * 2:2]
    margin = jnp.minimum(tallies[giver] - 1, limit - tallies[receiver]) // 2
    margin = jnp.where((giver == order[0]) | (receiver == order[0]) | (tallies[receiver] == 0), 0, jnp.maximum(margin, 0))
    moved = jax.random.randint(jax.random.fold_in(own, 4), (amount // 2,), 0, 1 << 20) % (margin + 1)
    tallies = tallies.at[giver].add(-moved).at[receiver].add(moved)
    members = jnp.searchsorted(jnp.cumsum(tallies), jnp.arange(rows * top), side="right").astype(jnp.int32)
    listing = members.reshape(top, rows).T
    listing = listing[jax.random.permutation(jax.random.fold_in(own, 1), rows)]
    rotation = jax.random.randint(jax.random.fold_in(own, 2), (rows, 1), 0, top)
    return jnp.take_along_axis(listing, (jnp.arange(top)[None, :] + rotation) % top, axis=1)


def shares(amount, total, limit, slope, full):
    loads = [(1 << 20) // math.isqrt(rank ** slope) + 1 for rank in range(1, amount + 1)]
    largest = limit if full else min(limit, max(-(-total // amount), total * loads[0] // sum(loads)))
    least = 1 if total - largest >= amount - 1 else 0
    given, surplus = [largest] + [least] * (amount - 1), total - largest - least * (amount - 1)
    while surplus > 0:
        free = [i for i in range(1, amount) if given[i] < largest] or [i for i in range(1, amount) if given[i] < limit]
        mass, remaining = sum([loads[i] for i in free]), surplus
        for i in free:
            more = min(limit - given[i], max(1, remaining * loads[i] // mass), surplus)
            given[i] = given[i] + more
            surplus = surplus - more
    return np.array(given)


def bell_draw(key, extent, scale, limit, split=(), held_as=jnp.bfloat16):
    drawn = scale * jax.random.normal(key, extent, jnp.float32)
    if split:
        drawn = drawn * level_of(key, extent, split, -0.22, 0.18)
    return jnp.clip(drawn, -limit, limit).astype(held_as)


def setup_inputs(seed: int = 0, part: int = 0) -> dict:
    keys = jax.random.split(jax.random.key(seed), 6)
    part_splits = jax.random.split(jax.random.fold_in(keys[5], part), 6)
    w_up = bell_draw(keys[0], (SECTIONS, EXPERTS * DW, FF), FF ** -0.5, 0.15625, ((0, 2), (1, 64)))
    saved_rows = bell_draw(part_splits[1], (SECTIONS, TOKENS, DW), 1.0, 6.0, ((0, 2), (1, 64)))
    hidden_grad = bell_draw(part_splits[2], (SECTIONS, TOKENS, TOPK, FF), 1.0, 6.0, ((0, 2), (1, 64)))
    expert_ids_keys = jax.random.split(jax.random.fold_in(part_splits[3], 1), SECTIONS * TOKENS // TOK)
    expert_ids_turns = jax.random.permutation(jax.random.fold_in(part_splits[3], 3), SECTIONS * TOKENS // TOK)
    expert_ids = jax.vmap(lambda own, number: deal_out(jax.random.fold_in(part_splits[3], 2), own, number, TOK, EXPERTS, TOPK, CAP, 2))(expert_ids_keys, expert_ids_turns).reshape((SECTIONS, TOKENS, TOPK))
    route_weight = jnp.clip(jnp.exp(math.log(1.0) - 2.3025851 * jax.random.uniform(part_splits[4], (SECTIONS, TOKENS, TOPK), jnp.float32) ** level_of(part_splits[4], (SECTIONS, TOKENS, TOPK), ((0, 2), (1, 64)), -0.2, 0.2)), 0.1, 1.0)
    return dict(w_up=w_up, saved_rows=saved_rows, hidden_grad=hidden_grad, expert_ids=expert_ids, route_weight=route_weight)


loss_scale_inverse = 0.0625


def one_segment(segment_args):
    segment_weight, segment_rows, segment_grad, segment_ids, segment_route = segment_args
    scaled = (segment_route[:, :, None] * segment_grad.astype(jnp.float32)).astype(jnp.bfloat16)
    row_grad = jnp.zeros((segment_rows.shape[0], DW), jnp.float32)
    weight_grads = []
    for expert in range(EXPERTS):
        route_mask = segment_ids == expert
        chosen_mask = jnp.any(route_mask, axis=1)
        picked = jnp.sum(jnp.where(route_mask[:, :, None], scaled.astype(jnp.float32), jnp.float32(0.0)), axis=1).astype(jnp.bfloat16)
        partial_value = jnp.dot(picked, segment_weight[expert].T, preferred_element_type=jnp.float32)
        partial_value = partial_value.astype(jnp.bfloat16).astype(jnp.float32)
        row_grad = row_grad + jnp.where(chosen_mask[:, None], partial_value, jnp.float32(0.0))
        masked_rows = jnp.where(chosen_mask[:, None], segment_rows, jnp.zeros_like(segment_rows))
        summed = jnp.dot(masked_rows.T, picked, preferred_element_type=jnp.float32)
        weight_grads.append((summed * loss_scale_inverse).astype(jnp.bfloat16))
    return jnp.concatenate(weight_grads, 0), row_grad.astype(jnp.bfloat16)


def reference(w_up, saved_rows, hidden_grad, expert_ids, route_weight):
    weights = w_up.reshape(SECTIONS, EXPERTS, DW, FF)
    weight_grad, row_grad = lax.map(one_segment, (weights, saved_rows, hidden_grad, expert_ids, route_weight))
    upstream = jnp.concatenate([row_grad[1:], jnp.zeros_like(row_grad[:1])], 0)
    return weight_grad, upstream
```

```python
import jax
import jax.numpy as jnp
from jax import lax
from jax.sharding import Mesh, PartitionSpec as P

loss_scale_inverse = 0.0625
bf16 = jnp.bfloat16
f32 = jnp.float32
ZY = ("z", "y")
CHUNKS = 2
TOKEN_PAIRS = [(0, 1), (1, 0), (2, 3), (3, 2)]
FEATURE_PAIRS = [(0, 3), (3, 0), (1, 2), (2, 1)]


def dot(a, b, dims):
    return lax.dot_general(a, b, (dims, ((), ())), preferred_element_type=f32)


def positions(ids, experts):
    chosen = jnp.any(ids[:, None, :, :] == jnp.arange(experts, dtype=ids.dtype)[None, :, None, None], axis=3)
    tokens = ids.shape[1]
    row = lax.broadcasted_iota(jnp.int32, (tokens, tokens), 0)
    col = lax.broadcasted_iota(jnp.int32, (tokens, tokens), 1)
    earlier = (row < col).astype(bf16)
    slot = dot(chosen.astype(bf16), earlier, ((2,), (0,)))
    return chosen, slot.astype(jnp.int32)


def body(w_up, saved_rows, hidden_grad, expert_ids, route_weight):
    experts = lax.axis_size("z") * lax.axis_size("y")
    x = lax.axis_index("x")
    me = lax.axis_index("z") * lax.axis_size("y") + lax.axis_index("y")
    tokens = saved_rows.shape[1]
    width = saved_rows.shape[2]
    top = hidden_grad.shape[2]
    hidden = hidden_grad.shape[3]
    quarter = width // 4
    half = width // 2
    capacity = 3 * tokens * top // (2 * experts)
    part = hidden // CHUNKS

    w_own = w_up[0]
    w_other = lax.ppermute(w_own, "x", FEATURE_PAIRS)

    def features(a, q):
        return lax.dynamic_slice_in_dim(a, q * quarter, quarter, 1)

    rows = saved_rows[0]
    ids = expert_ids[0]
    mate = jnp.bitwise_xor(x, 1)
    for_mate = jnp.concatenate(
        [features(rows, mate), features(rows, 3 - mate)], axis=1
    )
    id_wide = jnp.pad(ids.T.astype(bf16), ((0, 0), (0, half - tokens)))
    out_rows = jnp.concatenate([for_mate, id_wide], axis=0)
    mate_rows = lax.ppermute(out_rows, "x", TOKEN_PAIRS)
    mine = jnp.concatenate([features(rows, x), features(rows, 3 - x)], axis=1)
    mate_ids_t = mate_rows[tokens:, :tokens]
    id_both = jnp.concatenate(
        [ids.T.astype(bf16), mate_ids_t], axis=1
    )
    id_both = jnp.pad(id_both, ((0, 0), (0, half - 2 * tokens)))
    block = jnp.concatenate([mine, mate_rows[:tokens], id_both], axis=0)
    gathered = lax.all_gather(block, ZY, tiled=False)
    gathered = gathered.reshape(experts, 2 * tokens + top, half)

    both_ids = jnp.stack([ids, mate_ids_t.T.astype(jnp.int32)])
    chosen, slot = positions(both_ids, experts)
    slots = jnp.arange(capacity, dtype=jnp.int32)
    place_tok = jnp.logical_and(
        chosen[:, :, None, :], slot[:, :, None, :] == slots[None, None, :, None]
    ).astype(bf16)
    place_tok = place_tok.reshape(2, experts * capacity, tokens)
    hit = ids[None, :, :] == jnp.arange(experts, dtype=jnp.int32)[:, None, None]
    place = jnp.logical_and(
        hit[:, None, :, :], (slot[0][:, None, :] == slots[None, :, None])[:, :, :, None]
    ).astype(bf16)
    place = place.reshape(experts * capacity, tokens * top)
    scaled = (route_weight[0][:, :, None] * hidden_grad[0].astype(f32)).astype(bf16)
    scaled = scaled.reshape(tokens * top, hidden)

    own_grad, mate_grad = [], []
    for c in range(CHUNKS):
        packed = dot(place, scaled[:, c * part : (c + 1) * part], ((1,), (0,))).astype(bf16)
        got = lax.all_to_all(
            packed.reshape(experts, capacity, part), ZY, 0, 0, tiled=True
        ).reshape(experts * capacity, part)
        own_grad.append(got)
        mate_grad.append(lax.ppermute(got, "x", TOKEN_PAIRS))

    def route_grad(grads):
        outs = []
        for w in (w_own, w_other):
            total = dot(grads[0], w[:, :part], ((1,), (1,)))
            for c in range(1, CHUNKS):
                total = total + dot(grads[c], w[:, c * part : (c + 1) * part], ((1,), (1,)))
            outs.append(total.astype(bf16))
        out = jnp.concatenate(outs, axis=1).reshape(experts, capacity, half)
        back = lax.all_to_all(out, ZY, 0, 0, tiled=True)
        return back.reshape(experts * capacity, half)

    back_own = route_grad(own_grad)
    sum_own = dot(place_tok[0], back_own, ((0,), (0,))).astype(bf16)
    back_mate = route_grad(mate_grad)
    sum_mate = dot(place_tok[1], back_mate, ((0,), (0,))).astype(bf16)

    to_own = [(4 + i, i) for i in range(4)]
    to_mate = [(4 + i, j) for i, j in TOKEN_PAIRS]
    up_own = lax.ppermute(sum_own, ("section", "x"), to_own)
    up_mate = lax.ppermute(sum_mate, ("section", "x"), to_mate)
    pieces = []
    for q in range(4):
        pieces.append(
            jnp.where(
                q == x,
                up_own[:, :quarter],
                jnp.where(
                    q == 3 - x,
                    up_own[:, quarter:],
                    jnp.where(q == mate, up_mate[:, :quarter], up_mate[:, quarter:]),
                ),
            )
        )
    upstream = jnp.concatenate(pieces, axis=1)

    all_ids = gathered[:, 2 * tokens :, : 2 * tokens]
    named = jnp.any(all_ids == me.astype(bf16), axis=1).reshape(experts, 2, tokens)
    row = lax.broadcasted_iota(jnp.int32, (tokens, tokens), 0)
    col = lax.broadcasted_iota(jnp.int32, (tokens, tokens), 1)
    where = dot(named.astype(bf16), (row < col).astype(bf16), ((2,), (0,))).astype(jnp.int32)
    pick = jnp.logical_and(
        named[:, :, None, :], where[:, :, None, :] == slots[None, None, :, None]
    ).astype(bf16)
    plane_rows = []
    for p in range(2):
        plane = gathered[:, p * tokens : (p + 1) * tokens]
        plane_rows.append(
            lax.dot_general(
                pick[:, p], plane, (((2,), (1,)), ((0,), (0,))), preferred_element_type=f32
            )
            .astype(bf16)
            .reshape(experts * capacity, half)
        )
    outs = []
    for c in range(CHUNKS):
        def partial(lo):
            total = dot(plane_rows[0][:, lo : lo + quarter], own_grad[c], ((0,), (0,)))
            return total + dot(plane_rows[1][:, lo : lo + quarter], mate_grad[c], ((0,), (0,)))

        theirs = lax.ppermute(partial(quarter).astype(bf16), "x", FEATURE_PAIRS)
        summed = partial(0) + theirs.astype(f32)
        outs.append((summed * loss_scale_inverse).astype(bf16))
    weight_grad = jnp.concatenate(outs, axis=1)
    return weight_grad[None], upstream[None]


def solution(mesh):
    grid = Mesh(mesh.devices.reshape(2, 4, 4, 4), ("section", "z", "y", "x"))
    expert = ("z", "y", "x")
    return jax.shard_map(
        body,
        mesh=grid,
        in_specs=(
            P("section", expert, None),
            P("section", expert, None),
            P("section", expert, None, None),
            P("section", expert, None),
            P("section", expert, None),
        ),
        out_specs=(P("section", expert, None), P("section", expert, None)),
        check_vma=False,
    )
```

```python
import jax
import jax.numpy as jnp
from jax import lax
from jax.sharding import Mesh, PartitionSpec as P

loss_scale_inverse = 0.0625
bf16 = jnp.bfloat16
f32 = jnp.float32
ZY = ("z", "y")
STEPS = (
    (("z", 1), ("z", 3), ("y", 1), ("y", 3)),
    (("y", 3), ("y", 1), ("z", 3), ("z", 1)),
)
TO_RIGHT = [(i, (i + 1) % 4) for i in range(4)]
TO_LEFT = [(i, (i + 3) % 4) for i in range(4)]


def dot(a, b, dims):
    return lax.dot_general(a, b, (dims, ((), ())), preferred_element_type=f32)


def gather_plane(block, steps):
    kept = block[None]
    for i, (axis, flip) in enumerate(steps):
        got = lax.ppermute(kept, axis, [(j, j ^ flip) for j in range(4)])
        if i == len(steps) - 1:
            return kept, got
        kept = jnp.concatenate([kept, got], axis=0)


def sources(steps):
    out = [0]
    for axis, flip in steps:
        mask = flip * 4 if axis == "z" else flip
        out = out + [o ^ mask for o in out]
    return out


def body(w_up, saved_rows, hidden_grad, expert_ids, route_weight):
    experts = lax.axis_size("z") * lax.axis_size("y")
    x = lax.axis_index("x")
    me = lax.axis_index("z") * lax.axis_size("y") + lax.axis_index("y")
    tokens = saved_rows.shape[1]
    width = saved_rows.shape[2]
    top = hidden_grad.shape[2]
    hidden = hidden_grad.shape[3]
    quarter = width // 4
    half = width // 2
    capacity = 3 * tokens * top // (2 * experts)
    slots = experts * capacity

    w = w_up[0]
    w_right = lax.ppermute(w, "x", TO_LEFT)
    w_left = lax.ppermute(w, "x", TO_RIGHT)
    mid = quarter // 2
    w_far_a = lax.ppermute(w_right[:mid], "x", TO_LEFT)
    w_far_b = lax.ppermute(w_left[mid:], "x", TO_RIGHT)

    rows = saved_rows[0]
    ids = expert_ids[0]
    ids_t = ids.T
    id_rows = jnp.pad(ids_t.astype(bf16), ((0, 0), (0, half - tokens)))
    first = gather_plane(jnp.concatenate([rows[:, :half], id_rows], axis=0), STEPS[0])
    second = gather_plane(rows[:, half:], STEPS[1])

    names = jnp.arange(experts, dtype=jnp.int32)
    row = lax.broadcasted_iota(jnp.int32, (tokens, tokens), 0)
    col = lax.broadcasted_iota(jnp.int32, (tokens, tokens), 1)
    earlier = (row < col).astype(bf16)
    chosen = jnp.any(ids_t[:, None, :] == names[None, :, None], axis=0)
    slot = dot(chosen.astype(bf16), earlier, ((1,), (0,))).astype(jnp.int32)
    target_t = jnp.where(chosen, slot, -1)
    target = jnp.sum(
        jnp.where(ids_t[:, None, :] == names[None, :, None], slot[None] + capacity * names[None, :, None], 0), axis=1
    )
    target = target.T.reshape(1, tokens * top)
    place = (lax.broadcasted_iota(jnp.int32, (slots, 1), 0) == target).astype(bf16)
    scaled = (route_weight[0][:, :, None] * hidden_grad[0].astype(f32)).astype(bf16)
    scaled = scaled.reshape(tokens * top, hidden)
    packed = dot(place, scaled, ((1,), (0,))).astype(bf16).reshape(experts, capacity, hidden)
    grads = lax.all_to_all(packed, ZY, 0, 0, tiled=True).reshape(slots, hidden)

    outs = [
        dot(grads, piece, ((1,), (1,))).astype(bf16)
        for piece in (w, w_right, w_far_a, w_far_b, w_left)
    ]
    routed = jnp.concatenate(outs, axis=1).reshape(experts, capacity, width)
    back = lax.all_to_all(routed, ZY, 0, 0, tiled=True).reshape(slots, width)
    place_tok = (
        (lax.broadcasted_iota(jnp.int32, (1, capacity, 1), 1) == target_t[:, None, :])
        .astype(bf16)
        .reshape(slots, tokens)
    )
    turned = dot(place_tok, back, ((0,), (0,))).astype(bf16)
    turned = lax.ppermute(turned, "section", [(1, 0)])
    upstream = lax.dynamic_slice_in_dim(
        jnp.concatenate([turned, turned], axis=1), (4 - x) * quarter, width, 1
    )

    ids_in = jnp.concatenate([a[:, tokens:, :tokens] for a in first], axis=0)
    named = jnp.any(ids_in == me.astype(bf16), axis=1)
    where = dot(named.astype(bf16), earlier, ((1,), (0,))).astype(jnp.int32)
    froms = [sources(steps) for steps in STEPS]
    base = (jnp.array(froms[0], jnp.int32) ^ me) * capacity
    goal = jnp.where(named, where + base[:, None], -1)
    goals = [goal, jnp.stack([goal[froms[0].index(s)] for s in froms[1]])]
    picked = []
    for goal_h, pieces in zip(goals, (first, second)):
        total = 0.0
        for i, piece in enumerate(pieces):
            n = piece.shape[0]
            line = goal_h[i * n : (i + 1) * n].reshape(1, n * tokens)
            pick = (lax.broadcasted_iota(jnp.int32, (slots, 1), 0) == line).astype(bf16)
            total = total + dot(pick, piece[:, :tokens].reshape(n * tokens, half), ((1,), (0,)))
        picked.append(total.astype(bf16))
    picked = jnp.concatenate(picked + picked, axis=1)
    turned_rows = lax.dynamic_slice_in_dim(picked, x * quarter, width, 1)

    def partial(lo, hi):
        return dot(turned_rows[:, lo:hi], grads, ((0,), (0,)))

    a, b = 2 * quarter, 2 * quarter + mid
    far_a = lax.ppermute(partial(a, b).astype(bf16), "x", TO_RIGHT)
    far_b = lax.ppermute(partial(b, b + mid).astype(bf16), "x", TO_LEFT)
    right_b = lax.ppermute(partial(quarter + mid, 2 * quarter).astype(bf16), "x", TO_RIGHT)
    left_a = lax.ppermute(partial(3 * quarter, 3 * quarter + mid).astype(bf16), "x", TO_LEFT)
    right_a = partial(quarter, quarter + mid) + far_a.astype(f32)
    left_b = partial(3 * quarter + mid, width) + far_b.astype(f32)
    right_a = lax.ppermute(right_a.astype(bf16), "x", TO_RIGHT)
    left_b = lax.ppermute(left_b.astype(bf16), "x", TO_LEFT)
    top_half = partial(0, mid) + left_a.astype(f32) + right_a.astype(f32)
    low_half = partial(mid, quarter) + left_b.astype(f32) + right_b.astype(f32)
    weight_grad = jnp.concatenate([top_half, low_half], axis=0) * loss_scale_inverse
    return weight_grad.astype(bf16)[None], upstream[None]


def solution(mesh):
    grid = Mesh(mesh.devices.reshape(2, 4, 4, 4), ("section", "z", "y", "x"))
    expert = ("z", "y", "x")
    return jax.shard_map(
        body,
        mesh=grid,
        in_specs=(
            P("section", expert, None),
            P("section", expert, None),
            P("section", expert, None, None),
            P("section", expert, None),
            P("section", expert, None),
        ),
        out_specs=(P("section", expert, None), P("section", expert, None)),
        check_vma=False,
    )
```

```python
import jax
import jax.numpy as jnp
from jax import lax
from jax.sharding import Mesh, PartitionSpec as P

loss_scale_inverse = 0.0625
bf16 = jnp.bfloat16
f32 = jnp.float32
ZY = ("z", "y")
TO_RIGHT = [(i, (i + 1) % 4) for i in range(4)]
TO_LEFT = [(i, (i + 3) % 4) for i in range(4)]


FLIP_1 = [(i, i ^ 1) for i in range(4)]
FLIP_3 = [(i, i ^ 3) for i in range(4)]
MATES = [(4 * z + i, 4 * z + (i ^ (1 if z < 2 else 3))) for z in range(4) for i in range(4)]


def dot(a, b, dims):
    return lax.dot_general(a, b, (dims, ((), ())), preferred_element_type=f32)


def body(w_up, saved_rows, hidden_grad, expert_ids, route_weight):
    experts = lax.axis_size("z") * lax.axis_size("y")
    x = lax.axis_index("x")
    me = lax.axis_index("z") * lax.axis_size("y") + lax.axis_index("y")
    tokens = saved_rows.shape[1]
    width = saved_rows.shape[2]
    top = hidden_grad.shape[2]
    hidden = hidden_grad.shape[3]
    quarter = width // 4
    half = width // 2
    capacity = 3 * tokens * top // (2 * experts)
    slots = experts * capacity

    w = w_up[0]
    mid = quarter // 2
    right_a = lax.ppermute(w[:mid], "x", TO_LEFT)
    left_b = lax.ppermute(w[mid:], "x", TO_RIGHT)
    right_b = lax.ppermute(w[mid:], "x", TO_LEFT)
    left_a = lax.ppermute(w[:mid], "x", TO_RIGHT)
    far_a = lax.ppermute(right_a, "x", TO_LEFT)
    far_b = lax.ppermute(left_b, "x", TO_RIGHT)

    low = lax.axis_index("z") < 2
    other = jnp.where(low, x ^ 3, x ^ 1)
    mate = jnp.where(low, x ^ 1, x ^ 3)

    def features(q, r):
        parts = [lax.dynamic_slice_in_dim(saved_rows[0], i * quarter, quarter, 1) for i in (q, r)]
        return jnp.concatenate(parts, axis=1)

    ids = expert_ids[0]
    ids_t = ids.T
    ids_16 = ids_t.astype(bf16)
    lent = jnp.concatenate([features(mate, x ^ 2), jnp.pad(ids_16, ((0, 0), (0, half - tokens)))], axis=0)
    lent = lax.ppermute(lent, ("z", "x"), MATES)
    ids_pair = jnp.concatenate([ids_16, lent[tokens:, :tokens]], axis=1)
    ids_pair = jnp.pad(ids_pair, ((0, 0), (0, half - 2 * tokens)))
    gathered = lax.all_gather(
        jnp.concatenate([features(x, other), lent[:tokens], ids_pair], axis=0), ZY
    )

    names = jnp.arange(experts, dtype=jnp.int32)
    row = lax.broadcasted_iota(jnp.int32, (tokens, tokens), 0)
    col = lax.broadcasted_iota(jnp.int32, (tokens, tokens), 1)
    earlier = (row < col).astype(bf16)
    chosen = jnp.any(ids_t[:, None, :] == names[None, :, None], axis=0)
    slot = dot(chosen.astype(bf16), earlier, ((1,), (0,))).astype(jnp.int32)
    target_t = jnp.where(chosen, slot, -1)
    target = jnp.sum(
        jnp.where(ids_t[:, None, :] == names[None, :, None], slot[None] + capacity * names[None, :, None], 0), axis=1
    )
    target = target.T.reshape(1, tokens * top)
    place = (lax.broadcasted_iota(jnp.int32, (slots, 1), 0) == target).astype(bf16)
    scaled = (route_weight[0][:, :, None] * hidden_grad[0].astype(f32)).astype(bf16)
    scaled = scaled.reshape(tokens * top, hidden)
    packed = dot(place, scaled, ((1,), (0,))).astype(bf16).reshape(experts, capacity, hidden)
    arrived = lax.all_to_all(packed, ZY, 0, 0, tiled=True).reshape(slots, hidden)

    weights = jnp.concatenate([w, right_a, right_b, far_a, far_b, left_a, left_b], axis=0)
    weights, grads = lax.optimization_barrier((weights, arrived))
    routed = dot(grads, weights, ((1,), (1,))).astype(bf16).reshape(experts, capacity, width)
    back = lax.all_to_all(routed, ZY, 0, 0, tiled=True).reshape(slots, width)
    place_tok = (
        (lax.broadcasted_iota(jnp.int32, (1, capacity, 1), 1) == target_t[:, None, :])
        .astype(bf16)
        .reshape(slots, tokens)
    )
    turned = dot(place_tok, back, ((0,), (0,))).astype(bf16)
    turned = lax.ppermute(turned, "section", [(1, 0)])
    upstream = lax.dynamic_slice_in_dim(
        jnp.concatenate([turned, turned], axis=1), (4 - x) * quarter, width, 1
    )

    named = jnp.any(gathered[:, 2 * tokens :, : 2 * tokens] == me.astype(bf16), axis=1)
    where = dot(named.reshape(2 * experts, tokens).astype(bf16), earlier, ((1,), (0,))).astype(jnp.int32)
    where = where.reshape(experts, 2 * tokens)
    where = where + capacity * (lax.broadcasted_iota(jnp.int32, (1, 2 * tokens), 1) // tokens)
    where = jnp.pad(jnp.where(named, where, -1), ((0, 0), (0, top)), constant_values=-1)
    pick = (lax.broadcasted_iota(jnp.int32, (1, 2 * capacity, 1), 1) == where[:, None, :]).astype(bf16)
    picked = lax.dot_general(
        pick, gathered, (((2,), (1,)), ((0,), (0,))), preferred_element_type=f32
    ).astype(bf16)
    own = 0.0
    fars = []
    for s, flips in ((0, (FLIP_1, FLIP_3)), (1, (FLIP_3, FLIP_1))):
        held = arrived[s * slots // 2 : (s + 1) * slots // 2]
        both = jnp.concatenate(
            [a.reshape(experts // 2, capacity, hidden) for a in (held, lax.ppermute(held, "x", flips[0]))], axis=1
        ).reshape(slots, hidden)
        mine = picked[s * experts // 2 : (s + 1) * experts // 2].reshape(slots, half)
        far = dot(mine[:, quarter:], both, ((0,), (0,))).astype(bf16)
        fars.append(lax.ppermute(far, "x", flips[1]))
        own = own + dot(mine[:, :quarter], both, ((0,), (0,)))
    weight_grad = (own + fars[0].astype(f32) + fars[1].astype(f32)) * loss_scale_inverse
    return weight_grad.astype(bf16)[None], upstream[None]


def solution(mesh):
    grid = Mesh(mesh.devices.reshape(2, 4, 4, 4), ("section", "z", "y", "x"))
    expert = ("z", "y", "x")
    return jax.shard_map(
        body,
        mesh=grid,
        in_specs=(
            P("section", expert, None),
            P("section", expert, None),
            P("section", expert, None, None),
            P("section", expert, None),
            P("section", expert, None),
        ),
        out_specs=(P("section", expert, None), P("section", expert, None)),
        check_vma=False,
    )
```

```python
import functools

import jax
import jax.numpy as jnp
from jax import lax
from jax.experimental import pallas as pl
from jax.experimental.pallas import tpu as pltpu
from jax.sharding import Mesh, PartitionSpec as P

loss_scale_inverse = 0.0625
bf16 = jnp.bfloat16
f32 = jnp.float32
ZY = ("z", "y")
TO_RIGHT = [(i, (i + 1) % 4) for i in range(4)]
TO_LEFT = [(i, (i + 3) % 4) for i in range(4)]


FLIP_1 = [(i, i ^ 1) for i in range(4)]
FLIP_3 = [(i, i ^ 3) for i in range(4)]
MATES = [(4 * z + i, 4 * z + (i ^ (1 if z < 2 else 3))) for z in range(4) for i in range(4)]


def dot(a, b, dims):
    return lax.dot_general(a, b, (dims, ((), ())), preferred_element_type=f32)


def pack_kernel(capacity, experts, ids_ref, weight_ref, grad_ref, out_ref, target_ref, route_ref):
    tokens, top = ids_ref.shape
    routes = tokens * top

    @pl.when(pl.program_id(0) == 0)
    def _():
        ids = ids_ref[...]
        names = lax.broadcasted_iota(jnp.int32, (tokens, experts), 1)
        hits = [ids[:, k : k + 1] == names for k in range(top)]
        chosen = jnp.zeros((tokens, experts), f32)
        for hit in hits:
            chosen = chosen + jnp.where(hit, 1.0, 0.0)
        row = lax.broadcasted_iota(jnp.int32, (tokens, tokens), 0)
        col = lax.broadcasted_iota(jnp.int32, (tokens, tokens), 1)
        earlier = jnp.where(col < row, 1.0, 0.0).astype(bf16)
        slot = jnp.dot(earlier, chosen.astype(bf16), preferred_element_type=f32)
        mine = jnp.zeros((tokens, top), f32)
        order = lax.broadcasted_iota(jnp.int32, (tokens, top), 1)
        for k, hit in enumerate(hits):
            one = jnp.sum(jnp.where(hit, slot, 0.0), axis=1, keepdims=True)
            mine = jnp.where(order == k, one, mine)
        spread = jnp.where(
            lax.broadcasted_iota(jnp.int32, (top, routes), 0)
            == lax.broadcasted_iota(jnp.int32, (top, routes), 1) % top,
            1.0,
            0.0,
        ).astype(bf16)
        here = (
            lax.broadcasted_iota(jnp.int32, (tokens, routes), 0)
            == lax.broadcasted_iota(jnp.int32, (tokens, routes), 1) // top
        )

        def as_row(a):
            wide = jnp.dot(a.astype(bf16), spread, preferred_element_type=f32)
            return jnp.sum(jnp.where(here, wide, 0.0), axis=0, keepdims=True)

        target = as_row(mine) + capacity * as_row(ids.astype(f32))
        target_ref[...] = jnp.broadcast_to(target.astype(jnp.int32), target_ref.shape)
        owner = jnp.where(
            lax.broadcasted_iota(jnp.int32, (routes, tokens), 0) // top
            == lax.broadcasted_iota(jnp.int32, (routes, tokens), 1),
            1.0,
            0.0,
        )
        wide = lax.dot_general(
            owner, weight_ref[...], (((1,), (0,)), ((), ())),
            precision=lax.Precision.HIGHEST, preferred_element_type=f32,
        )
        rank = lax.broadcasted_iota(jnp.int32, (routes, top), 0) % top
        wide = jnp.where(lax.broadcasted_iota(jnp.int32, (routes, top), 1) == rank, wide, 0.0)
        route_ref[...] = jnp.broadcast_to(jnp.sum(wide, axis=1, keepdims=True), route_ref.shape)

    slots = experts * capacity
    scaled = (route_ref[:, :1] * grad_ref[...].astype(f32)).astype(bf16)
    place = jnp.where(
        lax.broadcasted_iota(jnp.int32, (slots, routes), 0) == target_ref[:1, :], 1.0, 0.0
    ).astype(bf16)
    out_ref[...] = jnp.dot(place, scaled, preferred_element_type=f32).astype(bf16)


def pack(ids, weights, grads, capacity, experts):
    routes, hidden = grads.shape
    part = hidden // 3
    slots = experts * capacity
    return pl.pallas_call(
        functools.partial(pack_kernel, capacity, experts),
        grid=(3,),
        in_specs=[
            pl.BlockSpec(ids.shape, lambda i: (0, 0)),
            pl.BlockSpec(weights.shape, lambda i: (0, 0)),
            pl.BlockSpec((routes, part), lambda i: (0, i)),
        ],
        out_specs=pl.BlockSpec((slots, part), lambda i: (0, i)),
        out_shape=jax.ShapeDtypeStruct((slots, hidden), bf16),
        scratch_shapes=[pltpu.VMEM((8, routes), jnp.int32), pltpu.VMEM((routes, 128), f32)],
        compiler_params=pltpu.CompilerParams(vmem_limit_bytes=16 << 20),
        cost_estimate=pl.CostEstimate(flops=2 * slots * routes * hidden, bytes_accessed=4 << 20, transcendentals=0),
    )(ids, weights, grads)


def route_kernel(grads, weights, out_hbm, out, sems):
    part = weights.shape[0] // 4
    copies = []
    for i in range(4):
        cols = pl.ds(i * part, part)
        out[:, cols] = lax.dot_general(
            grads[...], weights[cols, :], (((1,), (1,)), ((), ())), preferred_element_type=f32
        ).astype(bf16)
        copies.append(pltpu.make_async_copy(out.at[:, cols], out_hbm.at[:, cols], sems.at[i]))
        copies[-1].start()
    for copy in copies:
        copy.wait()


def route_product(grads, weights):
    slots, hidden = grads.shape
    width = weights.shape[0]
    vmem = pl.BlockSpec(memory_space=pltpu.VMEM)
    return pl.pallas_call(
        route_kernel,
        in_specs=[vmem, vmem],
        out_specs=pl.BlockSpec(memory_space=pltpu.HBM),
        out_shape=jax.ShapeDtypeStruct((slots, width), bf16),
        scratch_shapes=[pltpu.VMEM((slots, width), bf16), pltpu.SemaphoreType.DMA((4,))],
        compiler_params=pltpu.CompilerParams(vmem_limit_bytes=24 << 20),
        cost_estimate=pl.CostEstimate(flops=1, bytes_accessed=1, transcendentals=0),
    )(grads, weights)


def sum_kernel(own_ref, far_a, far_b, out_ref):
    total = own_ref[...] + far_a[...].astype(f32) + far_b[...].astype(f32)
    out_ref[...] = (total * loss_scale_inverse).astype(bf16)


def scaled_sum(own, far_a, far_b):
    rows, hidden = own.shape
    block = pl.BlockSpec((rows // 4, hidden), lambda i: (i, 0))
    return pl.pallas_call(
        sum_kernel,
        grid=(4,),
        in_specs=[block] * 3,
        out_specs=block,
        out_shape=jax.ShapeDtypeStruct((rows, hidden), bf16),
        compiler_params=pltpu.CompilerParams(vmem_limit_bytes=16 << 20),
    )(own, far_a, far_b)


def rows_kernel(capacity, me_ref, rows_hbm, grads_hbm, lent_0, lent_1, far_a, far_b, own_hbm,
                rows, grads, lent, packed, far, own, sems, out_sems):
    experts, span, half = rows.shape
    slots, hidden = grads.shape
    tokens = (span - 16) // 2
    quarter = half // 2
    hs = slots // 2
    in_copies = [
        pltpu.make_async_copy(rows_hbm, rows, sems.at[0]),
        pltpu.make_async_copy(grads_hbm, grads, sems.at[1]),
    ]
    at = 0
    for i, part in enumerate((lent_0, lent_1)):
        n = part.shape[0]
        in_copies.append(pltpu.make_async_copy(part, lent.at[pl.ds(at, n)], sems.at[2 + i]))
        at += n
    for copy in in_copies:
        copy.start()
    row = lax.broadcasted_iota(jnp.int32, (2 * tokens, 2 * tokens), 0)
    col = lax.broadcasted_iota(jnp.int32, (2 * tokens, 2 * tokens), 1)
    same = (row < tokens) == (col < tokens)
    earlier = jnp.where(jnp.logical_and(row < col, same), 1.0, 0.0).astype(bf16)
    me = me_ref[0].astype(f32)
    place = lax.broadcasted_iota(jnp.int32, (1, 2 * tokens), 1)
    base = jnp.where(place < tokens, 0, capacity)
    in_copies[0].wait()
    named = []
    for s in range(experts):
        ids = rows[s, 2 * tokens :, : 2 * tokens].astype(f32)
        named.append(jnp.max(jnp.where(ids == me, 1.0, 0.0), axis=0, keepdims=True))
    named = jnp.concatenate(named, axis=0)
    where = jnp.dot(named.astype(bf16), earlier, preferred_element_type=f32).astype(jnp.int32)
    where = jnp.where(named > 0.5, where + base, -1)
    line = lax.broadcasted_iota(jnp.int32, (2 * capacity, 2 * tokens), 0)
    for s in range(experts):
        pick = jnp.where(line == where[s : s + 1, :], 1.0, 0.0).astype(bf16)
        got = jnp.dot(pick, rows[s, : 2 * tokens, :], preferred_element_type=f32).astype(bf16)
        packed[0, s * capacity : (s + 1) * capacity, :] = got[:capacity]
        packed[1, s * capacity : (s + 1) * capacity, :] = got[capacity:]
    for copy in in_copies[1:]:
        copy.wait()
    tn = (((0,), (0,)), ((), ()))
    part = hidden // 3
    out_copies = []
    for g, out in enumerate((far_a, far_b)):
        span_g = slice(g * hs, (g + 1) * hs)
        for c in range(3):
            cols = slice(c * part, (c + 1) * part)
            sums = lax.dot_general(
                packed[0, span_g, quarter:], grads[span_g, cols], tn, preferred_element_type=f32
            ) + lax.dot_general(
                packed[1, span_g, quarter:], lent[span_g, cols], tn, preferred_element_type=f32
            )
            far[g, :, cols] = sums.astype(bf16)
        out_copies.append(pltpu.make_async_copy(far.at[g], out, out_sems.at[g]))
        out_copies[-1].start()
    own[...] = packed[:, :, :quarter]
    out_copies.append(pltpu.make_async_copy(own, own_hbm, out_sems.at[2]))
    out_copies[-1].start()
    for copy in out_copies:
        copy.wait()


def rows_product(me, rows, grads, lent, capacity):
    experts, span, half = rows.shape
    slots, hidden = grads.shape
    quarter = half // 2
    any_space = pl.BlockSpec(memory_space=pl.ANY)
    return pl.pallas_call(
        functools.partial(rows_kernel, capacity),
        in_specs=[pl.BlockSpec(memory_space=pltpu.SMEM)] + [any_space] * 4,
        out_specs=[pl.BlockSpec(memory_space=pltpu.HBM)] * 2 + [any_space],
        out_shape=[
            jax.ShapeDtypeStruct((quarter, hidden), bf16),
            jax.ShapeDtypeStruct((quarter, hidden), bf16),
            jax.ShapeDtypeStruct((2, slots, quarter), bf16),
        ],
        scratch_shapes=[
            pltpu.VMEM(rows.shape, bf16),
            pltpu.VMEM((slots, hidden), bf16),
            pltpu.VMEM((slots, hidden), bf16),
            pltpu.VMEM((2, slots, half), bf16),
            pltpu.VMEM((2, quarter, hidden), bf16),
            pltpu.VMEM((2, slots, quarter), bf16),
            pltpu.SemaphoreType.DMA((4,)),
            pltpu.SemaphoreType.DMA((3,)),
        ],
        compiler_params=pltpu.CompilerParams(vmem_limit_bytes=24 << 20),
        cost_estimate=pl.CostEstimate(
            flops=60 * slots * quarter * hidden, bytes_accessed=16 << 20, transcendentals=0
        ),
    )(me, rows, grads, *lent)


def body(w_up, saved_rows, hidden_grad, expert_ids, route_weight):
    experts = lax.axis_size("z") * lax.axis_size("y")
    x = lax.axis_index("x")
    me = lax.axis_index("z") * lax.axis_size("y") + lax.axis_index("y")
    tokens = saved_rows.shape[1]
    width = saved_rows.shape[2]
    top = hidden_grad.shape[2]
    hidden = hidden_grad.shape[3]
    quarter = width // 4
    half = width // 2
    capacity = 3 * tokens * top // (2 * experts)
    slots = experts * capacity

    w = w_up[0]
    mid = quarter // 2
    right_a = lax.ppermute(w[:mid], "x", TO_LEFT)
    left_b = lax.ppermute(w[mid:], "x", TO_RIGHT)
    right_b = lax.ppermute(w[mid:], "x", TO_LEFT)
    left_a = lax.ppermute(w[:mid], "x", TO_RIGHT)

    low = lax.axis_index("z") < 2
    other = jnp.where(low, x ^ 3, x ^ 1)
    mate = jnp.where(low, x ^ 1, x ^ 3)

    def features(q, r):
        parts = [lax.dynamic_slice_in_dim(saved_rows[0], i * quarter, quarter, 1) for i in (q, r)]
        return jnp.concatenate(parts, axis=1)

    ids = expert_ids[0]
    ids_t = ids.T
    ids_16 = ids_t.astype(bf16)
    lent = jnp.concatenate([features(mate, x ^ 2), jnp.pad(ids_16, ((0, 0), (0, half - tokens)))], axis=0)
    lent = lax.ppermute(lent, ("z", "x"), MATES)
    ids_pair = jnp.concatenate([ids_16, lent[tokens:, :tokens]], axis=1)
    ids_pair = jnp.pad(ids_pair, ((0, 16 - top), (0, half - 2 * tokens)), constant_values=-1)
    gathered = lax.all_gather(
        jnp.concatenate([features(x, other), lent[:tokens], ids_pair], axis=0), ZY
    )

    names = jnp.arange(experts, dtype=jnp.int32)
    row = lax.broadcasted_iota(jnp.int32, (tokens, tokens), 0)
    col = lax.broadcasted_iota(jnp.int32, (tokens, tokens), 1)
    earlier = (row < col).astype(bf16)
    chosen = jnp.any(ids_t[:, None, :] == names[None, :, None], axis=0)
    slot = dot(chosen.astype(bf16), earlier, ((1,), (0,))).astype(jnp.int32)
    target_t = jnp.where(chosen, slot, -1)
    scaled = hidden_grad[0].reshape(tokens * top, hidden)
    packed = pack(ids, route_weight[0], scaled, capacity, experts).reshape(experts, capacity, hidden)
    packed, right_a, left_b = lax.optimization_barrier((packed, right_a, left_b))
    far_a = lax.ppermute(right_a, "x", TO_LEFT)
    far_b = lax.ppermute(left_b, "x", TO_RIGHT)
    arrived = lax.all_to_all(packed, ZY, 0, 0, tiled=True).reshape(slots, hidden)

    weights = jnp.concatenate([w, right_a, right_b, far_a, far_b, left_a, left_b], axis=0)
    held, weights = lax.optimization_barrier((arrived, weights))
    hs = slots // 2
    lent = [lax.ppermute(held[:hs], "x", FLIP_1), lax.ppermute(held[hs:], "x", FLIP_3)]
    routed = route_product(held, weights)
    routed = routed.reshape(experts, capacity, width)
    back = lax.all_to_all(routed, ZY, 0, 0, tiled=True).reshape(slots, width)
    far_3, far_1, mine = rows_product(me[None], gathered, held, lent, capacity)
    target_t, far_3, far_1 = lax.optimization_barrier((target_t, far_3, far_1))
    place_tok = (
        (lax.broadcasted_iota(jnp.int32, (1, capacity, 1), 1) == target_t[:, None, :])
        .astype(bf16)
        .reshape(slots, tokens)
    )
    turned = dot(place_tok, back, ((0,), (0,))).astype(bf16)
    turned = lax.ppermute(turned, "section", [(1, 0)])
    upstream = lax.dynamic_slice_in_dim(
        jnp.concatenate([turned, turned], axis=1), (4 - x) * quarter, width, 1
    )

    far_3 = lax.ppermute(far_3, "x", FLIP_3)
    far_1 = lax.ppermute(far_1, "x", FLIP_1)
    own = dot(mine[0], held, ((0,), (0,)))
    lo = 0
    for part in lent:
        hi = lo + part.shape[0]
        own = own + dot(mine[1, lo:hi], part, ((0,), (0,)))
        lo = hi
    return scaled_sum(own, far_3, far_1)[None], upstream[None]


def solution(mesh):
    grid = Mesh(mesh.devices.reshape(2, 4, 4, 4), ("section", "z", "y", "x"))
    expert = ("z", "y", "x")
    return jax.shard_map(
        body,
        mesh=grid,
        in_specs=(
            P("section", expert, None),
            P("section", expert, None),
            P("section", expert, None, None),
            P("section", expert, None),
            P("section", expert, None),
        ),
        out_specs=(P("section", expert, None), P("section", expert, None)),
        check_vma=False,
    )
```

```python
import functools

import jax
import jax.numpy as jnp
from jax import lax
from jax.experimental import pallas as pl
from jax.experimental.pallas import tpu as pltpu
from jax.sharding import Mesh, PartitionSpec as P

loss_scale_inverse = 0.0625
bf16 = jnp.bfloat16
f32 = jnp.float32
ZY = ("z", "y")
TO_RIGHT = [(i, (i + 1) % 4) for i in range(4)]
TO_LEFT = [(i, (i + 3) % 4) for i in range(4)]


FLIP_1 = [(i, i ^ 1) for i in range(4)]
FLIP_3 = [(i, i ^ 3) for i in range(4)]
MATES = [(4 * z + i, 4 * z + (i ^ (1 if z < 2 else 3))) for z in range(4) for i in range(4)]


def dot(a, b, dims):
    return lax.dot_general(a, b, (dims, ((), ())), preferred_element_type=f32)


def pack_kernel(capacity, experts, ids_ref, weight_ref, grad_ref, out_ref, target_ref, route_ref):
    tokens, top = ids_ref.shape
    routes = tokens * top

    @pl.when(pl.program_id(0) == 0)
    def _():
        ids = ids_ref[...]
        names = lax.broadcasted_iota(jnp.int32, (tokens, experts), 1)
        hits = [ids[:, k : k + 1] == names for k in range(top)]
        chosen = jnp.zeros((tokens, experts), f32)
        for hit in hits:
            chosen = chosen + jnp.where(hit, 1.0, 0.0)
        row = lax.broadcasted_iota(jnp.int32, (tokens, tokens), 0)
        col = lax.broadcasted_iota(jnp.int32, (tokens, tokens), 1)
        earlier = jnp.where(col < row, 1.0, 0.0).astype(bf16)
        slot = jnp.dot(earlier, chosen.astype(bf16), preferred_element_type=f32)
        mine = jnp.zeros((tokens, top), f32)
        order = lax.broadcasted_iota(jnp.int32, (tokens, top), 1)
        for k, hit in enumerate(hits):
            one = jnp.sum(jnp.where(hit, slot, 0.0), axis=1, keepdims=True)
            mine = jnp.where(order == k, one, mine)
        spread = jnp.where(
            lax.broadcasted_iota(jnp.int32, (top, routes), 0)
            == lax.broadcasted_iota(jnp.int32, (top, routes), 1) % top,
            1.0,
            0.0,
        ).astype(bf16)
        here = (
            lax.broadcasted_iota(jnp.int32, (tokens, routes), 0)
            == lax.broadcasted_iota(jnp.int32, (tokens, routes), 1) // top
        )

        def as_row(a):
            wide = jnp.dot(a.astype(bf16), spread, preferred_element_type=f32)
            return jnp.sum(jnp.where(here, wide, 0.0), axis=0, keepdims=True)

        target = as_row(mine) + capacity * as_row(ids.astype(f32))
        target_ref[...] = jnp.broadcast_to(target.astype(jnp.int32), target_ref.shape)
        owner = jnp.where(
            lax.broadcasted_iota(jnp.int32, (routes, tokens), 0) // top
            == lax.broadcasted_iota(jnp.int32, (routes, tokens), 1),
            1.0,
            0.0,
        )
        wide = lax.dot_general(
            owner, weight_ref[...], (((1,), (0,)), ((), ())),
            precision=lax.Precision.HIGHEST, preferred_element_type=f32,
        )
        rank = lax.broadcasted_iota(jnp.int32, (routes, top), 0) % top
        wide = jnp.where(lax.broadcasted_iota(jnp.int32, (routes, top), 1) == rank, wide, 0.0)
        route_ref[...] = jnp.broadcast_to(jnp.sum(wide, axis=1, keepdims=True), route_ref.shape)

    slots = experts * capacity
    scaled = (route_ref[:, :1] * grad_ref[...].astype(f32)).astype(bf16)
    place = jnp.where(
        lax.broadcasted_iota(jnp.int32, (slots, routes), 0) == target_ref[:1, :], 1.0, 0.0
    ).astype(bf16)
    out_ref[...] = jnp.dot(place, scaled, preferred_element_type=f32).astype(bf16)


def pack(ids, weights, grads, capacity, experts):
    routes, hidden = grads.shape
    part = hidden // 3
    slots = experts * capacity
    return pl.pallas_call(
        functools.partial(pack_kernel, capacity, experts),
        grid=(3,),
        in_specs=[
            pl.BlockSpec(ids.shape, lambda i: (0, 0)),
            pl.BlockSpec(weights.shape, lambda i: (0, 0)),
            pl.BlockSpec((routes, part), lambda i: (0, i)),
        ],
        out_specs=pl.BlockSpec((slots, part), lambda i: (0, i)),
        out_shape=jax.ShapeDtypeStruct((slots, hidden), bf16),
        scratch_shapes=[pltpu.VMEM((8, routes), jnp.int32), pltpu.VMEM((routes, 128), f32)],
        compiler_params=pltpu.CompilerParams(vmem_limit_bytes=16 << 20),
        cost_estimate=pl.CostEstimate(flops=1, bytes_accessed=1, transcendentals=0),
    )(ids, weights, grads)


def halves_kernel(grads_ref, low_ref, high_ref):
    n = low_ref.shape[0]
    low_ref[...] = grads_ref[:n, :]
    high_ref[...] = grads_ref[n:, :]


def halves(grads):
    slots, hidden = grads.shape
    vmem = pl.BlockSpec(memory_space=pltpu.VMEM)
    return pl.pallas_call(
        halves_kernel,
        in_specs=[vmem],
        out_specs=[vmem, vmem],
        out_shape=[jax.ShapeDtypeStruct((slots // 2, hidden), bf16)] * 2,
        compiler_params=pltpu.CompilerParams(vmem_limit_bytes=12 << 20),
        cost_estimate=pl.CostEstimate(flops=45 << 30, bytes_accessed=4 << 20, transcendentals=0),
    )(grads)


def sum_kernel(own_ref, far_a, far_b, out_ref):
    total = own_ref[...] + far_a[...].astype(f32) + far_b[...].astype(f32)
    out_ref[...] = (total * loss_scale_inverse).astype(bf16)


def scaled_sum(own, far_a, far_b):
    rows, hidden = own.shape
    block = pl.BlockSpec((rows // 4, hidden), lambda i: (i, 0))
    return pl.pallas_call(
        sum_kernel,
        grid=(4,),
        in_specs=[block] * 3,
        out_specs=block,
        out_shape=jax.ShapeDtypeStruct((rows, hidden), bf16),
        compiler_params=pltpu.CompilerParams(vmem_limit_bytes=16 << 20),
    )(own, far_a, far_b)


def rows_kernel(capacity, me_ref, rows_hbm, grads_hbm, lent_0, lent_1, far_a, far_b, own_hbm,
                rows, grads, lent, packed, far, own, sems, out_sems):
    experts, span, half = rows.shape
    slots, hidden = grads.shape
    tokens = (span - 16) // 2
    quarter = half // 2
    hs = slots // 2
    in_copies = [
        pltpu.make_async_copy(rows_hbm, rows, sems.at[0]),
        pltpu.make_async_copy(grads_hbm, grads, sems.at[1]),
    ]
    at = 0
    for i, part in enumerate((lent_0, lent_1)):
        n = part.shape[0]
        in_copies.append(pltpu.make_async_copy(part, lent.at[pl.ds(at, n)], sems.at[2 + i]))
        at += n
    for copy in in_copies:
        copy.start()
    row = lax.broadcasted_iota(jnp.int32, (2 * tokens, 2 * tokens), 0)
    col = lax.broadcasted_iota(jnp.int32, (2 * tokens, 2 * tokens), 1)
    same = (row < tokens) == (col < tokens)
    earlier = jnp.where(jnp.logical_and(row < col, same), 1.0, 0.0).astype(bf16)
    me = me_ref[0].astype(f32)
    place = lax.broadcasted_iota(jnp.int32, (1, 2 * tokens), 1)
    base = jnp.where(place < tokens, 0, capacity)
    in_copies[0].wait()
    named = []
    for s in range(experts):
        ids = rows[s, 2 * tokens :, : 2 * tokens].astype(f32)
        named.append(jnp.max(jnp.where(ids == me, 1.0, 0.0), axis=0, keepdims=True))
    named = jnp.concatenate(named, axis=0)
    where = jnp.dot(named.astype(bf16), earlier, preferred_element_type=f32).astype(jnp.int32)
    where = jnp.where(named > 0.5, where + base, -1)
    line = lax.broadcasted_iota(jnp.int32, (2 * capacity, 2 * tokens), 0)
    for s in range(experts):
        pick = jnp.where(line == where[s : s + 1, :], 1.0, 0.0).astype(bf16)
        got = jnp.dot(pick, rows[s, : 2 * tokens, :], preferred_element_type=f32).astype(bf16)
        packed[0, s * capacity : (s + 1) * capacity, :] = got[:capacity]
        packed[1, s * capacity : (s + 1) * capacity, :] = got[capacity:]
    for copy in in_copies[1:]:
        copy.wait()
    tn = (((0,), (0,)), ((), ()))
    part = hidden // 3
    out_copies = []
    for g, out in enumerate((far_a, far_b)):
        span_g = slice(g * hs, (g + 1) * hs)
        for c in range(3):
            cols = slice(c * part, (c + 1) * part)
            sums = lax.dot_general(
                packed[0, span_g, quarter:], grads[span_g, cols], tn, preferred_element_type=f32
            ) + lax.dot_general(
                packed[1, span_g, quarter:], lent[span_g, cols], tn, preferred_element_type=f32
            )
            far[g, :, cols] = sums.astype(bf16)
        out_copies.append(pltpu.make_async_copy(far.at[g], out, out_sems.at[g]))
        out_copies[-1].start()
    own[...] = packed[:, :, :quarter]
    out_copies.append(pltpu.make_async_copy(own, own_hbm, out_sems.at[2]))
    out_copies[-1].start()
    for copy in out_copies:
        copy.wait()


def rows_product(me, rows, grads, lent, capacity):
    experts, span, half = rows.shape
    slots, hidden = grads.shape
    quarter = half // 2
    any_space = pl.BlockSpec(memory_space=pl.ANY)
    return pl.pallas_call(
        functools.partial(rows_kernel, capacity),
        in_specs=[pl.BlockSpec(memory_space=pltpu.SMEM)] + [any_space] * 4,
        out_specs=[pl.BlockSpec(memory_space=pltpu.HBM)] * 2 + [any_space],
        out_shape=[
            jax.ShapeDtypeStruct((quarter, hidden), bf16),
            jax.ShapeDtypeStruct((quarter, hidden), bf16),
            jax.ShapeDtypeStruct((2, slots, quarter), bf16),
        ],
        scratch_shapes=[
            pltpu.VMEM(rows.shape, bf16),
            pltpu.VMEM((slots, hidden), bf16),
            pltpu.VMEM((slots, hidden), bf16),
            pltpu.VMEM((2, slots, half), bf16),
            pltpu.VMEM((2, quarter, hidden), bf16),
            pltpu.VMEM((2, slots, quarter), bf16),
            pltpu.SemaphoreType.DMA((4,)),
            pltpu.SemaphoreType.DMA((3,)),
        ],
        compiler_params=pltpu.CompilerParams(vmem_limit_bytes=24 << 20),
        cost_estimate=pl.CostEstimate(
            flops=60 * slots * quarter * hidden, bytes_accessed=16 << 20, transcendentals=0
        ),
    )(me, rows, grads, *lent)


def body(w_up, saved_rows, hidden_grad, expert_ids, route_weight):
    experts = lax.axis_size("z") * lax.axis_size("y")
    x = lax.axis_index("x")
    me = lax.axis_index("z") * lax.axis_size("y") + lax.axis_index("y")
    tokens = saved_rows.shape[1]
    width = saved_rows.shape[2]
    top = hidden_grad.shape[2]
    hidden = hidden_grad.shape[3]
    quarter = width // 4
    half = width // 2
    capacity = 3 * tokens * top // (2 * experts)
    slots = experts * capacity

    w = w_up[0]
    mid = quarter // 2
    right_a = lax.ppermute(w[:mid], "x", TO_LEFT)
    left_b = lax.ppermute(w[mid:], "x", TO_RIGHT)
    right_b = lax.ppermute(w[mid:], "x", TO_LEFT)
    left_a = lax.ppermute(w[:mid], "x", TO_RIGHT)

    low = lax.axis_index("z") < 2
    other = jnp.where(low, x ^ 3, x ^ 1)
    mate = jnp.where(low, x ^ 1, x ^ 3)

    def features(q, r):
        parts = [lax.dynamic_slice_in_dim(saved_rows[0], i * quarter, quarter, 1) for i in (q, r)]
        return jnp.concatenate(parts, axis=1)

    ids = expert_ids[0]
    ids_t = ids.T
    ids_16 = ids_t.astype(bf16)
    lent = jnp.concatenate([features(mate, x ^ 2), jnp.pad(ids_16, ((0, 0), (0, half - tokens)))], axis=0)
    lent = lax.ppermute(lent, ("z", "x"), MATES)
    names = jnp.arange(experts, dtype=jnp.int32)
    row = lax.broadcasted_iota(jnp.int32, (tokens, tokens), 0)
    col = lax.broadcasted_iota(jnp.int32, (tokens, tokens), 1)
    earlier = (row < col).astype(bf16)
    chosen = jnp.any(ids_t[:, None, :] == names[None, :, None], axis=0)
    slot = dot(chosen.astype(bf16), earlier, ((1,), (0,))).astype(jnp.int32)
    target_t = jnp.where(chosen, slot, -1)
    scaled = hidden_grad[0].reshape(tokens * top, hidden)
    packed = pack(ids, route_weight[0], scaled, capacity, experts).reshape(experts, capacity, hidden)
    packed, lent = lax.optimization_barrier((packed, lent))
    ids_pair = jnp.concatenate([ids_16, lent[tokens:, :tokens]], axis=1)
    ids_pair = jnp.pad(ids_pair, ((0, 16 - top), (0, half - 2 * tokens)), constant_values=-1)
    block = jnp.concatenate([features(x, other), lent[:tokens], ids_pair], axis=0)

    packed, block = lax.optimization_barrier((packed, block))
    gathered = lax.all_gather(block, ZY)
    far_a = lax.ppermute(right_a, "x", TO_LEFT)
    far_b = lax.ppermute(left_b, "x", TO_RIGHT)
    arrived = lax.all_to_all(packed, ZY, 0, 0, tiled=True).reshape(slots, hidden)

    weights = jnp.concatenate([w, right_a, right_b, far_a, far_b, left_a, left_b], axis=0)
    held, weights = lax.optimization_barrier((arrived, weights))
    hs = slots // 2
    low_half, high_half = halves(held)
    lent = [lax.ppermute(low_half, "x", FLIP_1), lax.ppermute(high_half, "x", FLIP_3)]
    routed = dot(held, weights, ((1,), (1,))).astype(bf16)
    routed = routed.reshape(experts, capacity, width)
    back = lax.all_to_all(routed, ZY, 0, 0, tiled=True).reshape(slots, width)
    far_3, far_1, mine = rows_product(me[None], gathered, held, lent, capacity)
    far_3 = lax.ppermute(far_3, "x", FLIP_3)
    far_1 = lax.ppermute(far_1, "x", FLIP_1)
    own = dot(mine[0], held, ((0,), (0,)))
    lo = 0
    for part in lent:
        hi = lo + part.shape[0]
        own = own + dot(mine[1, lo:hi], part, ((0,), (0,)))
        lo = hi
    target_t, own = lax.optimization_barrier((target_t, own))
    place_tok = (
        (lax.broadcasted_iota(jnp.int32, (1, capacity, 1), 1) == target_t[:, None, :])
        .astype(bf16)
        .reshape(slots, tokens)
    )
    turned = dot(place_tok, back, ((0,), (0,))).astype(bf16)
    turned = lax.ppermute(turned, "section", [(1, 0)])
    upstream = lax.dynamic_slice_in_dim(
        jnp.concatenate([turned, turned], axis=1), (4 - x) * quarter, width, 1
    )

    return scaled_sum(own, far_3, far_1)[None], upstream[None]


def solution(mesh):
    grid = Mesh(mesh.devices.reshape(2, 4, 4, 4), ("section", "z", "y", "x"))
    expert = ("z", "y", "x")
    return jax.shard_map(
        body,
        mesh=grid,
        in_specs=(
            P("section", expert, None),
            P("section", expert, None),
            P("section", expert, None, None),
            P("section", expert, None),
            P("section", expert, None),
        ),
        out_specs=(P("section", expert, None), P("section", expert, None)),
        check_vma=False,
    )
```

```python
import functools

import jax
import jax.numpy as jnp
from jax import lax
from jax.experimental import pallas as pl
from jax.experimental.pallas import tpu as pltpu
from jax.sharding import Mesh, PartitionSpec as P

loss_scale_inverse = 0.0625
bf16 = jnp.bfloat16
f32 = jnp.float32
ZY = ("z", "y")
TO_RIGHT = [(i, (i + 1) % 4) for i in range(4)]
TO_LEFT = [(i, (i + 3) % 4) for i in range(4)]


FLIP_1 = [(i, i ^ 1) for i in range(4)]
FLIP_3 = [(i, i ^ 3) for i in range(4)]
MATES = [(4 * z + i, 4 * z + (i ^ (1 if z < 2 else 3))) for z in range(4) for i in range(4)]


def dot(a, b, dims):
    return lax.dot_general(a, b, (dims, ((), ())), preferred_element_type=f32)


def pack_kernel(capacity, experts, ids_ref, weight_ref, grad_ref, out_ref, target_ref, route_ref):
    tokens, top = ids_ref.shape
    routes = tokens * top

    @pl.when(pl.program_id(0) == 0)
    def _():
        ids = ids_ref[...]
        names = lax.broadcasted_iota(jnp.int32, (tokens, experts), 1)
        hits = [ids[:, k : k + 1] == names for k in range(top)]
        chosen = jnp.zeros((tokens, experts), f32)
        for hit in hits:
            chosen = chosen + jnp.where(hit, 1.0, 0.0)
        row = lax.broadcasted_iota(jnp.int32, (tokens, tokens), 0)
        col = lax.broadcasted_iota(jnp.int32, (tokens, tokens), 1)
        earlier = jnp.where(col < row, 1.0, 0.0).astype(bf16)
        slot = jnp.dot(earlier, chosen.astype(bf16), preferred_element_type=f32)
        mine = jnp.zeros((tokens, top), f32)
        order = lax.broadcasted_iota(jnp.int32, (tokens, top), 1)
        for k, hit in enumerate(hits):
            one = jnp.sum(jnp.where(hit, slot, 0.0), axis=1, keepdims=True)
            mine = jnp.where(order == k, one, mine)
        spread = jnp.where(
            lax.broadcasted_iota(jnp.int32, (top, routes), 0)
            == lax.broadcasted_iota(jnp.int32, (top, routes), 1) % top,
            1.0,
            0.0,
        ).astype(bf16)
        here = (
            lax.broadcasted_iota(jnp.int32, (tokens, routes), 0)
            == lax.broadcasted_iota(jnp.int32, (tokens, routes), 1) // top
        )

        def as_row(a):
            wide = jnp.dot(a.astype(bf16), spread, preferred_element_type=f32)
            return jnp.sum(jnp.where(here, wide, 0.0), axis=0, keepdims=True)

        target = as_row(mine) + capacity * as_row(ids.astype(f32))
        target_ref[...] = jnp.broadcast_to(target.astype(jnp.int32), target_ref.shape)
        owner = jnp.where(
            lax.broadcasted_iota(jnp.int32, (routes, tokens), 0) // top
            == lax.broadcasted_iota(jnp.int32, (routes, tokens), 1),
            1.0,
            0.0,
        )
        wide = lax.dot_general(
            owner, weight_ref[...], (((1,), (0,)), ((), ())),
            precision=lax.Precision.HIGHEST, preferred_element_type=f32,
        )
        rank = lax.broadcasted_iota(jnp.int32, (routes, top), 0) % top
        wide = jnp.where(lax.broadcasted_iota(jnp.int32, (routes, top), 1) == rank, wide, 0.0)
        route_ref[...] = jnp.broadcast_to(jnp.sum(wide, axis=1, keepdims=True), route_ref.shape)

    slots = experts * capacity
    scaled = (route_ref[:, :1] * grad_ref[...].astype(f32)).astype(bf16)
    place = jnp.where(
        lax.broadcasted_iota(jnp.int32, (slots, routes), 0) == target_ref[:1, :], 1.0, 0.0
    ).astype(bf16)
    out_ref[...] = jnp.dot(place, scaled, preferred_element_type=f32).astype(bf16)


def pack(ids, weights, grads, capacity, experts):
    routes, hidden = grads.shape
    part = hidden // 3
    slots = experts * capacity
    return pl.pallas_call(
        functools.partial(pack_kernel, capacity, experts),
        grid=(3,),
        in_specs=[
            pl.BlockSpec(ids.shape, lambda i: (0, 0)),
            pl.BlockSpec(weights.shape, lambda i: (0, 0)),
            pl.BlockSpec((routes, part), lambda i: (0, i)),
        ],
        out_specs=pl.BlockSpec((slots, part), lambda i: (0, i)),
        out_shape=jax.ShapeDtypeStruct((slots, hidden), bf16),
        scratch_shapes=[pltpu.VMEM((8, routes), jnp.int32), pltpu.VMEM((routes, 128), f32)],
        compiler_params=pltpu.CompilerParams(vmem_limit_bytes=16 << 20),
        cost_estimate=pl.CostEstimate(flops=1, bytes_accessed=1, transcendentals=0),
    )(ids, weights, grads)


def halves_kernel(grads_ref, low_ref, high_ref):
    n = low_ref.shape[0]
    low_ref[...] = grads_ref[:n, :]
    high_ref[...] = grads_ref[n:, :]


def halves(grads):
    slots, hidden = grads.shape
    vmem = pl.BlockSpec(memory_space=pltpu.VMEM)
    return pl.pallas_call(
        halves_kernel,
        in_specs=[vmem],
        out_specs=[vmem, vmem],
        out_shape=[jax.ShapeDtypeStruct((slots // 2, hidden), bf16)] * 2,
        compiler_params=pltpu.CompilerParams(vmem_limit_bytes=12 << 20),
        cost_estimate=pl.CostEstimate(flops=45 << 30, bytes_accessed=4 << 20, transcendentals=0),
    )(grads)


def sum_kernel(own_ref, far_a, far_b, out_ref):
    total = own_ref[...] + far_a[...].astype(f32) + far_b[...].astype(f32)
    out_ref[...] = (total * loss_scale_inverse).astype(bf16)


def scaled_sum(own, far_a, far_b):
    rows, hidden = own.shape
    block = pl.BlockSpec((rows // 4, hidden), lambda i: (i, 0))
    return pl.pallas_call(
        sum_kernel,
        grid=(4,),
        in_specs=[block] * 3,
        out_specs=block,
        out_shape=jax.ShapeDtypeStruct((rows, hidden), bf16),
        compiler_params=pltpu.CompilerParams(vmem_limit_bytes=16 << 20),
    )(own, far_a, far_b)


def pick_kernel(capacity, me_ref, rows, near, other):
    experts, span, half = rows.shape
    tokens = (span - 16) // 2
    quarter = half // 2
    row = lax.broadcasted_iota(jnp.int32, (2 * tokens, 2 * tokens), 0)
    col = lax.broadcasted_iota(jnp.int32, (2 * tokens, 2 * tokens), 1)
    same = (row < tokens) == (col < tokens)
    earlier = jnp.where(jnp.logical_and(row < col, same), 1.0, 0.0).astype(bf16)
    me = me_ref[0].astype(f32)
    place = lax.broadcasted_iota(jnp.int32, (1, 2 * tokens), 1)
    base = jnp.where(place < tokens, 0, capacity)
    named = []
    for s in range(experts):
        ids = rows[s, 2 * tokens :, : 2 * tokens].astype(f32)
        named.append(jnp.max(jnp.where(ids == me, 1.0, 0.0), axis=0, keepdims=True))
    named = jnp.concatenate(named, axis=0)
    where = jnp.dot(named.astype(bf16), earlier, preferred_element_type=f32).astype(jnp.int32)
    where = jnp.where(named > 0.5, where + base, -1)
    line = lax.broadcasted_iota(jnp.int32, (2 * capacity, 2 * tokens), 0)
    for s in range(experts):
        pick = jnp.where(line == where[s : s + 1, :], 1.0, 0.0).astype(bf16)
        got = jnp.dot(pick, rows[s, : 2 * tokens, :], preferred_element_type=f32).astype(bf16)
        here = pl.ds(s * capacity, capacity)
        for p in range(2):
            part = got[p * capacity : (p + 1) * capacity]
            near[p, here, :] = part[:, :quarter]
            other[p, here, :] = part[:, quarter:]


def pick_rows(me, rows, capacity):
    experts, span, half = rows.shape
    vmem = pl.BlockSpec(memory_space=pltpu.VMEM)
    out = jax.ShapeDtypeStruct((2, experts * capacity, half // 2), bf16)
    return pl.pallas_call(
        functools.partial(pick_kernel, capacity),
        in_specs=[pl.BlockSpec(memory_space=pltpu.SMEM), vmem],
        out_specs=[vmem, vmem],
        out_shape=[out, out],
        compiler_params=pltpu.CompilerParams(vmem_limit_bytes=20 << 20),
        cost_estimate=pl.CostEstimate(flops=1, bytes_accessed=1, transcendentals=0),
    )(me, rows)


def far_kernel(rows, grads, lent_a, lent_b, far_a, far_b):
    tn = (((0,), (0,)), ((), ()))
    hs, hidden = lent_a.shape
    part = hidden // 3
    for g, (lent, far) in enumerate(((lent_a, far_a), (lent_b, far_b))):
        span = pl.ds(g * hs, hs)
        for c in range(3):
            cols = pl.ds(c * part, part)
            sums = lax.dot_general(
                rows[0, span, :], grads[span, cols], tn, preferred_element_type=f32
            ) + lax.dot_general(rows[1, span, :], lent[:, cols], tn, preferred_element_type=f32)
            far[:, cols] = sums.astype(bf16)


def far_products(rows, grads, lent):
    slots, hidden = grads.shape
    quarter = rows.shape[2]
    vmem = pl.BlockSpec(memory_space=pltpu.VMEM)
    out = jax.ShapeDtypeStruct((quarter, hidden), bf16)
    return pl.pallas_call(
        far_kernel,
        in_specs=[vmem] * 4,
        out_specs=[vmem, vmem],
        out_shape=[out, out],
        compiler_params=pltpu.CompilerParams(vmem_limit_bytes=24 << 20),
        cost_estimate=pl.CostEstimate(
            flops=60 * slots * quarter * hidden, bytes_accessed=16 << 20, transcendentals=0
        ),
    )(rows, grads, *lent)


def body(w_up, saved_rows, hidden_grad, expert_ids, route_weight):
    experts = lax.axis_size("z") * lax.axis_size("y")
    x = lax.axis_index("x")
    me = lax.axis_index("z") * lax.axis_size("y") + lax.axis_index("y")
    tokens = saved_rows.shape[1]
    width = saved_rows.shape[2]
    top = hidden_grad.shape[2]
    hidden = hidden_grad.shape[3]
    quarter = width // 4
    half = width // 2
    capacity = 3 * tokens * top // (2 * experts)
    slots = experts * capacity

    w = w_up[0]
    mid = quarter // 2
    right_a = lax.ppermute(w[:mid], "x", TO_LEFT)
    left_b = lax.ppermute(w[mid:], "x", TO_RIGHT)
    right_b = lax.ppermute(w[mid:], "x", TO_LEFT)
    left_a = lax.ppermute(w[:mid], "x", TO_RIGHT)

    low = lax.axis_index("z") < 2
    other = jnp.where(low, x ^ 3, x ^ 1)
    mate = jnp.where(low, x ^ 1, x ^ 3)

    def features(q, r):
        parts = [lax.dynamic_slice_in_dim(saved_rows[0], i * quarter, quarter, 1) for i in (q, r)]
        return jnp.concatenate(parts, axis=1)

    ids = expert_ids[0]
    ids_t = ids.T
    ids_16 = ids_t.astype(bf16)
    lent = jnp.concatenate([features(mate, x ^ 2), jnp.pad(ids_16, ((0, 0), (0, half - tokens)))], axis=0)
    lent = lax.ppermute(lent, ("z", "x"), MATES)
    names = jnp.arange(experts, dtype=jnp.int32)
    row = lax.broadcasted_iota(jnp.int32, (tokens, tokens), 0)
    col = lax.broadcasted_iota(jnp.int32, (tokens, tokens), 1)
    earlier = (row < col).astype(bf16)
    chosen = jnp.any(ids_t[:, None, :] == names[None, :, None], axis=0)
    slot = dot(chosen.astype(bf16), earlier, ((1,), (0,))).astype(jnp.int32)
    target_t = jnp.where(chosen, slot, -1)
    scaled = hidden_grad[0].reshape(tokens * top, hidden)
    packed = pack(ids, route_weight[0], scaled, capacity, experts).reshape(experts, capacity, hidden)
    packed, lent = lax.optimization_barrier((packed, lent))
    ids_pair = jnp.concatenate([ids_16, lent[tokens:, :tokens]], axis=1)
    ids_pair = jnp.pad(ids_pair, ((0, 16 - top), (0, half - 2 * tokens)), constant_values=-1)
    block = jnp.concatenate([features(x, other), lent[:tokens], ids_pair], axis=0)

    packed, block = lax.optimization_barrier((packed, block))
    gathered = lax.all_gather(block, ZY)
    far_a = lax.ppermute(right_a, "x", TO_LEFT)
    far_b = lax.ppermute(left_b, "x", TO_RIGHT)
    arrived = lax.all_to_all(packed, ZY, 0, 0, tiled=True).reshape(slots, hidden)

    weights = jnp.concatenate([w, right_a, right_b, far_a, far_b, left_a, left_b], axis=0)
    held, weights = lax.optimization_barrier((arrived, weights))
    hs = slots // 2
    low_half, high_half = halves(held)
    lent = [lax.ppermute(low_half, "x", FLIP_1), lax.ppermute(high_half, "x", FLIP_3)]
    routed = dot(held, weights, ((1,), (1,))).astype(bf16)
    routed = routed.reshape(experts, capacity, width)
    back = lax.all_to_all(routed, ZY, 0, 0, tiled=True).reshape(slots, width)
    mine, other_rows = pick_rows(me[None], gathered, capacity)
    far_3, far_1 = far_products(other_rows, held, lent)
    far_3 = lax.ppermute(far_3, "x", FLIP_3)
    far_1 = lax.ppermute(far_1, "x", FLIP_1)
    own = dot(mine[0], held, ((0,), (0,)))
    lo = 0
    for part in lent:
        hi = lo + part.shape[0]
        own = own + dot(mine[1, lo:hi], part, ((0,), (0,)))
        lo = hi
    target_t, own = lax.optimization_barrier((target_t, own))
    place_tok = (
        (lax.broadcasted_iota(jnp.int32, (1, capacity, 1), 1) == target_t[:, None, :])
        .astype(bf16)
        .reshape(slots, tokens)
    )
    turned = dot(place_tok, back, ((0,), (0,))).astype(bf16)
    turned = lax.ppermute(turned, "section", [(1, 0)])
    upstream = lax.dynamic_slice_in_dim(
        jnp.concatenate([turned, turned], axis=1), (4 - x) * quarter, width, 1
    )

    return scaled_sum(own, far_3, far_1)[None], upstream[None]


def solution(mesh):
    grid = Mesh(mesh.devices.reshape(2, 4, 4, 4), ("section", "z", "y", "x"))
    expert = ("z", "y", "x")
    return jax.shard_map(
        body,
        mesh=grid,
        in_specs=(
            P("section", expert, None),
            P("section", expert, None),
            P("section", expert, None, None),
            P("section", expert, None),
            P("section", expert, None),
        ),
        out_specs=(P("section", expert, None), P("section", expert, None)),
        check_vma=False,
    )
```

```python
import functools

import jax
import jax.numpy as jnp
from jax import lax
from jax.experimental import pallas as pl
from jax.experimental.pallas import tpu as pltpu
from jax.sharding import Mesh, PartitionSpec as P

loss_scale_inverse = 0.0625
bf16 = jnp.bfloat16
f32 = jnp.float32
ZY = ("z", "y")
TO_RIGHT = [(i, (i + 1) % 4) for i in range(4)]
TO_LEFT = [(i, (i + 3) % 4) for i in range(4)]


FLIP_1 = [(i, i ^ 1) for i in range(4)]
FLIP_3 = [(i, i ^ 3) for i in range(4)]
MATES = [(4 * z + i, 4 * z + (i ^ (1 if z < 2 else 3))) for z in range(4) for i in range(4)]


def dot(a, b, dims):
    return lax.dot_general(a, b, (dims, ((), ())), preferred_element_type=f32)


def pack_kernel(capacity, experts, ids_ref, weight_ref, grad_ref, out_ref, target_ref, route_ref):
    tokens, top = ids_ref.shape
    routes = tokens * top

    @pl.when(pl.program_id(0) == 0)
    def _():
        ids = ids_ref[...]
        names = lax.broadcasted_iota(jnp.int32, (tokens, experts), 1)
        hits = [ids[:, k : k + 1] == names for k in range(top)]
        chosen = jnp.zeros((tokens, experts), f32)
        for hit in hits:
            chosen = chosen + jnp.where(hit, 1.0, 0.0)
        row = lax.broadcasted_iota(jnp.int32, (tokens, tokens), 0)
        col = lax.broadcasted_iota(jnp.int32, (tokens, tokens), 1)
        earlier = jnp.where(col < row, 1.0, 0.0).astype(bf16)
        slot = jnp.dot(earlier, chosen.astype(bf16), preferred_element_type=f32)
        mine = jnp.zeros((tokens, top), f32)
        order = lax.broadcasted_iota(jnp.int32, (tokens, top), 1)
        for k, hit in enumerate(hits):
            one = jnp.sum(jnp.where(hit, slot, 0.0), axis=1, keepdims=True)
            mine = jnp.where(order == k, one, mine)
        spread = jnp.where(
            lax.broadcasted_iota(jnp.int32, (top, routes), 0)
            == lax.broadcasted_iota(jnp.int32, (top, routes), 1) % top,
            1.0,
            0.0,
        ).astype(bf16)
        here = (
            lax.broadcasted_iota(jnp.int32, (tokens, routes), 0)
            == lax.broadcasted_iota(jnp.int32, (tokens, routes), 1) // top
        )

        def as_row(a):
            wide = jnp.dot(a.astype(bf16), spread, preferred_element_type=f32)
            return jnp.sum(jnp.where(here, wide, 0.0), axis=0, keepdims=True)

        target = as_row(mine) + capacity * as_row(ids.astype(f32))
        target_ref[...] = jnp.broadcast_to(target.astype(jnp.int32), target_ref.shape)
        owner = jnp.where(
            lax.broadcasted_iota(jnp.int32, (routes, tokens), 0) // top
            == lax.broadcasted_iota(jnp.int32, (routes, tokens), 1),
            1.0,
            0.0,
        )
        wide = lax.dot_general(
            owner, weight_ref[...], (((1,), (0,)), ((), ())),
            precision=lax.Precision.HIGHEST, preferred_element_type=f32,
        )
        rank = lax.broadcasted_iota(jnp.int32, (routes, top), 0) % top
        wide = jnp.where(lax.broadcasted_iota(jnp.int32, (routes, top), 1) == rank, wide, 0.0)
        route_ref[...] = jnp.broadcast_to(jnp.sum(wide, axis=1, keepdims=True), route_ref.shape)

    slots = experts * capacity
    scaled = (route_ref[:, :1] * grad_ref[...].astype(f32)).astype(bf16)
    place = jnp.where(
        lax.broadcasted_iota(jnp.int32, (slots, routes), 0) == target_ref[:1, :], 1.0, 0.0
    ).astype(bf16)
    out_ref[...] = jnp.dot(place, scaled, preferred_element_type=f32).astype(bf16)


def pack(ids, weights, grads, capacity, experts):
    routes, hidden = grads.shape
    part = hidden // 3
    slots = experts * capacity
    return pl.pallas_call(
        functools.partial(pack_kernel, capacity, experts),
        grid=(3,),
        in_specs=[
            pl.BlockSpec(ids.shape, lambda i: (0, 0)),
            pl.BlockSpec(weights.shape, lambda i: (0, 0)),
            pl.BlockSpec((routes, part), lambda i: (0, i)),
        ],
        out_specs=pl.BlockSpec((slots, part), lambda i: (0, i)),
        out_shape=jax.ShapeDtypeStruct((slots, hidden), bf16),
        scratch_shapes=[pltpu.VMEM((8, routes), jnp.int32), pltpu.VMEM((routes, 128), f32)],
        compiler_params=pltpu.CompilerParams(vmem_limit_bytes=16 << 20),
        cost_estimate=pl.CostEstimate(flops=1, bytes_accessed=1, transcendentals=0),
    )(ids, weights, grads)


def halves_kernel(grads_ref, low_ref, high_ref):
    n = low_ref.shape[0]
    low_ref[...] = grads_ref[:n, :]
    high_ref[...] = grads_ref[n:, :]


def halves(grads):
    slots, hidden = grads.shape
    vmem = pl.BlockSpec(memory_space=pltpu.VMEM)
    return pl.pallas_call(
        halves_kernel,
        in_specs=[vmem],
        out_specs=[vmem, vmem],
        out_shape=[jax.ShapeDtypeStruct((slots // 2, hidden), bf16)] * 2,
        compiler_params=pltpu.CompilerParams(vmem_limit_bytes=12 << 20),
        cost_estimate=pl.CostEstimate(flops=45 << 30, bytes_accessed=4 << 20, transcendentals=0),
    )(grads)


def sum_kernel(own_ref, far_a, far_b, out_ref):
    total = own_ref[...] + far_a[...].astype(f32) + far_b[...].astype(f32)
    out_ref[...] = (total * loss_scale_inverse).astype(bf16)


def scaled_sum(own, far_a, far_b):
    vmem = pl.BlockSpec(memory_space=pltpu.VMEM)
    return pl.pallas_call(
        sum_kernel,
        in_specs=[vmem] * 3,
        out_specs=vmem,
        out_shape=jax.ShapeDtypeStruct(own.shape, bf16),
        compiler_params=pltpu.CompilerParams(vmem_limit_bytes=16 << 20),
    )(own, far_a, far_b)


def pick_kernel(capacity, me_ref, rows, near, other):
    experts, span, half = rows.shape
    tokens = (span - 16) // 2
    quarter = half // 2
    row = lax.broadcasted_iota(jnp.int32, (2 * tokens, 2 * tokens), 0)
    col = lax.broadcasted_iota(jnp.int32, (2 * tokens, 2 * tokens), 1)
    same = (row < tokens) == (col < tokens)
    earlier = jnp.where(jnp.logical_and(row < col, same), 1.0, 0.0).astype(bf16)
    me = me_ref[0].astype(f32)
    place = lax.broadcasted_iota(jnp.int32, (1, 2 * tokens), 1)
    base = jnp.where(place < tokens, 0, capacity)
    named = []
    for s in range(experts):
        ids = rows[s, 2 * tokens :, : 2 * tokens].astype(f32)
        named.append(jnp.max(jnp.where(ids == me, 1.0, 0.0), axis=0, keepdims=True))
    named = jnp.concatenate(named, axis=0)
    where = jnp.dot(named.astype(bf16), earlier, preferred_element_type=f32).astype(jnp.int32)
    where = jnp.where(named > 0.5, where + base, -1)
    line = lax.broadcasted_iota(jnp.int32, (2 * capacity, 2 * tokens), 0)
    for s in range(experts):
        pick = jnp.where(line == where[s : s + 1, :], 1.0, 0.0).astype(bf16)
        got = jnp.dot(pick, rows[s, : 2 * tokens, :], preferred_element_type=f32).astype(bf16)
        here = pl.ds(s * capacity, capacity)
        for p in range(2):
            part = got[p * capacity : (p + 1) * capacity]
            near[p, here, :] = part[:, :quarter]
            other[p, here, :] = part[:, quarter:]


def pick_rows(me, rows, capacity):
    experts, span, half = rows.shape
    vmem = pl.BlockSpec(memory_space=pltpu.VMEM)
    out = jax.ShapeDtypeStruct((2, experts * capacity, half // 2), bf16)
    return pl.pallas_call(
        functools.partial(pick_kernel, capacity),
        in_specs=[pl.BlockSpec(memory_space=pltpu.SMEM), vmem],
        out_specs=[vmem, vmem],
        out_shape=[out, out],
        compiler_params=pltpu.CompilerParams(vmem_limit_bytes=20 << 20),
        cost_estimate=pl.CostEstimate(flops=1, bytes_accessed=1, transcendentals=0),
    )(me, rows)


def far_kernel(rows, grads, lent_a, lent_b, far_a, far_b):
    tn = (((0,), (0,)), ((), ()))
    hs, hidden = lent_a.shape
    part = hidden // 3
    for g, (lent, far) in enumerate(((lent_a, far_a), (lent_b, far_b))):
        span = pl.ds(g * hs, hs)
        for c in range(3):
            cols = pl.ds(c * part, part)
            sums = lax.dot_general(
                rows[0, span, :], grads[span, cols], tn, preferred_element_type=f32
            ) + lax.dot_general(rows[1, span, :], lent[:, cols], tn, preferred_element_type=f32)
            far[:, cols] = sums.astype(bf16)


def far_products(rows, grads, lent):
    slots, hidden = grads.shape
    quarter = rows.shape[2]
    vmem = pl.BlockSpec(memory_space=pltpu.VMEM)
    out = jax.ShapeDtypeStruct((quarter, hidden), bf16)
    return pl.pallas_call(
        far_kernel,
        in_specs=[vmem] * 4,
        out_specs=[vmem, vmem],
        out_shape=[out, out],
        compiler_params=pltpu.CompilerParams(vmem_limit_bytes=24 << 20),
        cost_estimate=pl.CostEstimate(
            flops=60 * slots * quarter * hidden, bytes_accessed=16 << 20, transcendentals=0
        ),
    )(rows, grads, *lent)


def body(w_up, saved_rows, hidden_grad, expert_ids, route_weight):
    experts = lax.axis_size("z") * lax.axis_size("y")
    x = lax.axis_index("x")
    me = lax.axis_index("z") * lax.axis_size("y") + lax.axis_index("y")
    tokens = saved_rows.shape[1]
    width = saved_rows.shape[2]
    top = hidden_grad.shape[2]
    hidden = hidden_grad.shape[3]
    quarter = width // 4
    half = width // 2
    capacity = 3 * tokens * top // (2 * experts)
    slots = experts * capacity

    w = w_up[0]
    mid = quarter // 2
    right_a = lax.ppermute(w[:mid], "x", TO_LEFT)
    left_b = lax.ppermute(w[mid:], "x", TO_RIGHT)
    right_b = lax.ppermute(w[mid:], "x", TO_LEFT)
    left_a = lax.ppermute(w[:mid], "x", TO_RIGHT)

    low = lax.axis_index("z") < 2
    other = jnp.where(low, x ^ 3, x ^ 1)
    mate = jnp.where(low, x ^ 1, x ^ 3)

    def features(q, r):
        parts = [lax.dynamic_slice_in_dim(saved_rows[0], i * quarter, quarter, 1) for i in (q, r)]
        return jnp.concatenate(parts, axis=1)

    ids = expert_ids[0]
    ids_t = ids.T
    ids_16 = ids_t.astype(bf16)
    lent = jnp.concatenate([features(mate, x ^ 2), jnp.pad(ids_16, ((0, 0), (0, half - tokens)))], axis=0)
    lent = lax.ppermute(lent, ("z", "x"), MATES)
    names = jnp.arange(experts, dtype=jnp.int32)
    row = lax.broadcasted_iota(jnp.int32, (tokens, tokens), 0)
    col = lax.broadcasted_iota(jnp.int32, (tokens, tokens), 1)
    earlier = (row < col).astype(bf16)
    chosen = jnp.any(ids_t[:, None, :] == names[None, :, None], axis=0)
    slot = dot(chosen.astype(bf16), earlier, ((1,), (0,))).astype(jnp.int32)
    target_t = jnp.where(chosen, slot, -1)
    scaled = hidden_grad[0].reshape(tokens * top, hidden)
    packed = pack(ids, route_weight[0], scaled, capacity, experts).reshape(experts, capacity, hidden)
    packed, lent = lax.optimization_barrier((packed, lent))
    ids_pair = jnp.concatenate([ids_16, lent[tokens:, :tokens]], axis=1)
    ids_pair = jnp.pad(ids_pair, ((0, 16 - top), (0, half - 2 * tokens)), constant_values=-1)
    block = jnp.concatenate([features(x, other), lent[:tokens], ids_pair], axis=0)

    packed, block = lax.optimization_barrier((packed, block))
    gathered = lax.all_gather(block, ZY)
    far_a = lax.ppermute(right_a, "x", TO_LEFT)
    far_b = lax.ppermute(left_b, "x", TO_RIGHT)
    arrived = lax.all_to_all(packed, ZY, 0, 0, tiled=True).reshape(slots, hidden)

    weights = jnp.concatenate([w, right_a, right_b, far_a, far_b, left_a, left_b], axis=0)
    held, weights = lax.optimization_barrier((arrived, weights))
    hs = slots // 2
    low_half, high_half = halves(held)
    lent = [lax.ppermute(low_half, "x", FLIP_1), lax.ppermute(high_half, "x", FLIP_3)]
    routed = dot(held, weights, ((1,), (1,))).astype(bf16)
    routed = routed.reshape(experts, capacity, width)
    back = lax.all_to_all(routed, ZY, 0, 0, tiled=True).reshape(slots, width)
    mine, other_rows = pick_rows(me[None], gathered, capacity)
    far_3, far_1 = far_products(other_rows, held, lent)
    far_3 = lax.ppermute(far_3, "x", FLIP_3)
    far_1 = lax.ppermute(far_1, "x", FLIP_1)
    own = dot(mine[0], held, ((0,), (0,)))
    lo = 0
    for part in lent:
        hi = lo + part.shape[0]
        own = own + dot(mine[1, lo:hi], part, ((0,), (0,)))
        lo = hi
    target_t, own = lax.optimization_barrier((target_t, own))
    place_tok = (
        (lax.broadcasted_iota(jnp.int32, (1, capacity, 1), 1) == target_t[:, None, :])
        .astype(bf16)
        .reshape(slots, tokens)
    )
    turned = dot(place_tok, back, ((0,), (0,))).astype(bf16)
    turned = lax.ppermute(turned, "section", [(1, 0)])
    upstream = lax.dynamic_slice_in_dim(
        jnp.concatenate([turned, turned], axis=1), (4 - x) * quarter, width, 1
    )

    return scaled_sum(own, far_3, far_1)[None], upstream[None]


def solution(mesh):
    grid = Mesh(mesh.devices.reshape(2, 4, 4, 4), ("section", "z", "y", "x"))
    expert = ("z", "y", "x")
    return jax.shard_map(
        body,
        mesh=grid,
        in_specs=(
            P("section", expert, None),
            P("section", expert, None),
            P("section", expert, None, None),
            P("section", expert, None),
            P("section", expert, None),
        ),
        out_specs=(P("section", expert, None), P("section", expert, None)),
        check_vma=False,
    )
```
